128 devices in a mesh: wide: 64 (over z, y, x), narrow: 2 (over core).
Axes of the slice: x: 4, y: 4, z: 4, core: 2. Of those that a mesh axis runs over, the one named last changes fastest.
Arguments:
- voltages: bfloat16 [1024, 2, 2, 779, 192], P(('narrow', 'wide')), may hold values from -8 to 8
- flags: int32 [512], replicated, may hold values 0 or 1
- tiles: int32 [10, 2], P('narrow'), may hold values from 0 to 3, as said below
Outputs:
- visibilities: float32 [10, 384, 2, 65536], P('narrow', 'wide')
The draws below stay inside these ranges and needn't reach their ends.
Inputs may be any that keep to these rules, and one draw needn't show every extreme that they name: `tiles`: every pair (r, c) with r >= c of the 4 groups stands exactly once in the whole list.
All inputs are finite; a program needn't handle non-finite values.
Results may differ from the reference program's by a relative error of at most 0.0006.
Values may be sent and summed in bfloat16 or wider, within the bound.
No kernel may reach another device: no remote copies, remote signals or barrier semaphores. Data moves between devices by JAX's collectives and lax.ppermute only.
A program may use at most 192 MiB of HBM per device.

```python
import jax
import jax.numpy as jnp
import numpy as np
from jax import lax

INPUTS = 1024
F = 192
TAPS = 12
COARSE = 2
S = 768
STATIONS = 512
FRAMES = 779
NGROUP = 4
TIN = 256
NTILE = 10


def draw_voltages(key, part):
    key = jax.random.fold_in(key, 11)
    shape_full = (INPUTS, COARSE, 2, FRAMES, F)
    sky_signal = jax.random.normal(jax.random.fold_in(key, 1), (COARSE, 2, FRAMES, F), jnp.float32)
    input_gains = 0.8 * jax.random.normal(jax.random.fold_in(key, 2), (INPUTS,), jnp.float32)
    noise_part = jax.random.normal(jax.random.fold_in(key, 3), shape_full, jnp.float32)
    values = input_gains[:, None, None, None, None] * sky_signal[None] + noise_part
    return jnp.clip(values, -8.0, 8.0).astype(jnp.bfloat16)


def draw_tiles(key, part):
    key = jax.random.fold_in(key, 23)
    lower_rows, lower_cols = np.tril_indices(NGROUP)
    pair_table = jnp.stack([jnp.asarray(lower_rows, jnp.int32), jnp.asarray(lower_cols, jnp.int32)], axis=1)
    shuffle_order = jax.random.permutation(key, NTILE)
    return pair_table[shuffle_order]


def set_ends(entries, own_key, least, largest):
    longest = entries.shape.index(max(entries.shape))
    spots = []
    for shift in (0, 1):
        where = [jax.random.randint(jax.random.fold_in(own_key, axis), (), 0, length) for axis, length in enumerate(entries.shape)]
        where[longest] = (where[longest] + shift) % entries.shape[longest]
        spots.append(tuple(where))
    return entries.at[spots[0]].set(least).at[spots[1]].set(largest)


def setup_inputs(seed: int = 0) -> dict:
    splits = jax.random.split(jax.random.key(seed), 4)
    voltages = draw_voltages(jax.random.fold_in(splits[3], 71), 0)
    flags = set_ends((jax.random.randint(splits[1], (STATIONS,), 0, 8) < 1).astype(jnp.int32), jax.random.fold_in(splits[1], 1), 0, 1)
    tiles = draw_tiles(jax.random.fold_in(splits[3], 71), 0)
    return {"voltages": voltages, "flags": flags, "tiles": tiles}


def prototype():
    length = TAPS * F
    sample = jnp.arange(length, dtype=jnp.float32)
    centre = (length - 1) / 2.0
    taper = jnp.sinc((sample - centre) / F)
    window = 0.5 - 0.5 * jnp.cos(2.0 * jnp.pi * (sample + 0.5) / length)
    shaped = taper * window
    shaped = shaped * jnp.sqrt(F / jnp.sum(shaped * shaped))
    return shaped.reshape(TAPS, F)

def reference(voltages, flags, tiles):
    filter_taps = prototype()
    framed = jnp.zeros((INPUTS, COARSE, 2, S, F), jnp.float32)
    for tap_index in range(TAPS):
        framed = framed + filter_taps[tap_index] * voltages[:, :, :, tap_index:tap_index + S, :].astype(jnp.float32)
    signal = lax.complex(framed[:, :, 0], framed[:, :, 1])
    transformed = jnp.fft.fft(signal, axis=-1) / jnp.sqrt(jnp.float32(F))
    both_parts = jnp.stack([jnp.real(transformed), jnp.imag(transformed)], axis=2)
    both_parts = jnp.transpose(both_parts, (0, 1, 4, 2, 3)).reshape(INPUTS, COARSE * F, 2, S)
    spectra = both_parts.astype(jnp.float32).astype(jnp.bfloat16)
    station_index = jnp.arange(INPUTS) // 2
    keep_input = (1 - flags[station_index]).astype(jnp.bfloat16)
    spectra = spectra * keep_input[:, None, None, None]
    flat_spectra = spectra.reshape(INPUTS, COARSE * F, 2 * S)

    def one_tile(tile_pair):
        rows_block = lax.dynamic_slice_in_dim(flat_spectra, (tile_pair[0] * TIN).astype(jnp.int32), TIN, 0).astype(jnp.float32)
        cols_block = lax.dynamic_slice_in_dim(flat_spectra, (tile_pair[1] * TIN).astype(jnp.int32), TIN, 0).astype(jnp.float32)
        rotated = jnp.concatenate([-cols_block[..., S:], cols_block[..., :S]], axis=-1)
        real_part = jnp.einsum('afs,bfs->fab', rows_block, cols_block)
        imag_part = jnp.einsum('afs,bfs->fab', rows_block, rotated)
        joined = jnp.stack([real_part, imag_part], axis=1) / S
        return joined.reshape(COARSE * F, 2, TIN * TIN)
    return lax.map(one_tile, tiles)
```

```python
import functools

import jax
import jax.numpy as jnp
import numpy as np
from jax import lax
from jax.experimental import pallas as pl
from jax.experimental.pallas import tpu as pltpu
from jax.sharding import PartitionSpec as P

F = 192
TAPS = 12
COARSE = 2
HEAD = 256
WIDE = 64
LOCAL = 8
PER = 6
LANES = 128
MADE = 15
TOGETHER = 4
SPLIT = (4, 2)
VMEM_BYTES = 60 * 2**20


def prototype():
    length = TAPS * F
    sample = np.arange(length, dtype=np.float64)
    centre = (length - 1) / 2.0
    taper = np.sinc((sample - centre) / F)
    window = 0.5 - 0.5 * np.cos(2.0 * np.pi * (sample + 0.5) / length)
    shaped = taper * window
    shaped = shaped * np.sqrt(F / np.sum(shaped * shaped))
    return shaped.reshape(TAPS, F)


def filter_table():
    taps = prototype().astype(np.float32)
    both = np.concatenate([taps, taps], axis=1)
    return np.ascontiguousarray(np.broadcast_to(both[:, None, :], (TAPS, 8, 2 * F)))


def transform_table():
    k = np.arange(F)
    angle = 2.0 * np.pi * ((k[:, None] * k[None, :]) % F) / F
    cosine, sine = np.cos(angle), np.sin(angle)
    real = np.concatenate([cosine, sine], axis=1)
    imag = np.concatenate([-sine, cosine], axis=1)
    rows = np.stack([real, imag], axis=1).reshape(2 * F, 2 * F) / np.sqrt(float(F))
    rows = rows.astype(np.float32)
    high = rows.astype(jnp.bfloat16)
    low = (rows - high.astype(np.float32)).astype(jnp.bfloat16)
    return np.concatenate([high, high, low], axis=1)


def spectra_kernel(first, count, split, flags_ref, volt_ref, taps_ref, table_ref, *rest):
    parts = len(split)
    outs, results = rest[:parts], rest[parts : 2 * parts]
    scratch = rest[2 * parts :]
    series, framed = scratch[:TOGETHER], scratch[TOGETHER : 2 * TOGETHER]
    volts, turned, in_sem, out_sem = scratch[2 * TOGETHER :]
    device = lax.axis_index("narrow") * WIDE + lax.axis_index("wide")
    slots = volts.shape[0]
    width = count + LANES
    total = COARSE * LOCAL
    span = volts.shape[-1]

    def incoming(n):
        slot = lax.rem(n, slots)
        source = volt_ref.at[lax.rem(n, LOCAL), n // LOCAL]
        if span < volt_ref.shape[-1]:
            source = source.at[:, :, pl.ds(0, span)]
        return pltpu.make_async_copy(source, volts.at[slot], in_sem.at[slot])

    def outgoing(c):
        half = WIDE // COARSE
        return [
            pltpu.make_async_copy(held.at[c], out.at[pl.ds(c * half, half)], out_sem.at[c, which])
            for which, (held, out) in enumerate(zip(results, outs))
        ]

    def transform(slot, i, series, framed):
        keep = (1 - flags_ref[(device * LOCAL + i) // 2]).astype(jnp.float32)
        for tile in range(width // LANES):
            start = first + tile * LANES
            stop = min(start + LANES, span)
            pieces = [volts[slot, p, :, start:stop].astype(jnp.float32) for p in range(2)]
            rows = jnp.concatenate(pieces, axis=0)
            for column in range(3):
                series[column, tile * LANES : tile * LANES + stop - start, :] = rows[
                    column * LANES : (column + 1) * LANES
                ].T
        for column in range(3):
            lanes = slice(column * LANES, (column + 1) * LANES)
            taps = [taps_ref[m, :, lanes] for m in range(TAPS)]
            for start in range(0, count, 64):
                value = None
                for m in range(TAPS):
                    tap = jnp.concatenate([taps[m]] * 8, axis=0)
                    term = tap * series[column, start + m : start + m + 64, :]
                    value = term if value is None else value + term
                top = value.astype(jnp.bfloat16)
                rest_part = (value - top.astype(jnp.float32)).astype(jnp.bfloat16)
                for third, half in enumerate((top, rest_part, top)):
                    at = third * 2 * F + column * LANES
                    framed[start : start + 64, at : at + LANES] = half
        product = lax.dot_general(
            table_ref[...], framed[...], (((1,), (1,)), ((), ())), preferred_element_type=jnp.float32
        )
        product = product * keep
        for tile in range(count // LANES):
            turned[tile, pl.ds(i, 2 * F, stride=LOCAL), :] = product[
                :, tile * LANES : (tile + 1) * LANES
            ]

    def step(q, carry):
        n = q * TOGETHER
        c = n // LOCAL

        @pl.when(n + TOGETHER < total)
        def _():
            for k in range(TOGETHER):
                incoming(n + TOGETHER + k).start()

        for k in range(TOGETHER):
            incoming(n + k).wait()
        for k in range(TOGETHER):
            transform(lax.rem(n + k, slots), lax.rem(n, LOCAL) + k, series[k], framed[k])

        @pl.when(lax.rem(n, LOCAL) == LOCAL - TOGETHER)
        def _():
            for tile in range(count // LANES):
                value = turned[tile].astype(jnp.bfloat16)
                value = value.reshape(WIDE // COARSE, PER * 2 * LOCAL, LANES)
                lanes = slice(tile * LANES, (tile + 1) * LANES)
                at = 0
                for held, channels in zip(results, split):
                    rows = channels * 2 * LOCAL
                    held[c, :, :, lanes] = value[:, at : at + rows, :]
                    at += rows
            for copy in outgoing(c):
                copy.start()

        return carry

    for k in range(TOGETHER):
        incoming(k).start()
    lax.fori_loop(0, total // TOGETHER, step, 0)
    for c in range(COARSE):
        for copy in outgoing(c):
            copy.wait()


def spectra(flags, voltages, taps, table, first, count, split):
    half = WIDE // COARSE
    reach = first + count + TAPS - 1
    span = min(-(-reach // LANES) * LANES, voltages.shape[-1])
    sizes = [(channels * 2 * LOCAL, count) for channels in split]
    smem, vmem, hbm = (
        pl.BlockSpec(memory_space=m) for m in (pltpu.SMEM, pltpu.VMEM, pl.ANY)
    )
    return pl.pallas_call(
        functools.partial(spectra_kernel, first, count, split),
        out_shape=[jax.ShapeDtypeStruct((WIDE,) + size, jnp.bfloat16) for size in sizes],
        in_specs=[smem, hbm, vmem, vmem],
        out_specs=[hbm] * len(split),
        scratch_shapes=[pltpu.VMEM((COARSE, half) + size, jnp.bfloat16) for size in sizes]
        + [pltpu.VMEM((3, count + LANES, LANES), jnp.float32)] * TOGETHER
        + [pltpu.VMEM((count, 6 * F), jnp.bfloat16)] * TOGETHER
        + [
            pltpu.VMEM((2 * TOGETHER, 2, F, span), jnp.bfloat16),
            pltpu.VMEM((count // LANES, 2 * F * LOCAL, LANES), jnp.float32),
            pltpu.SemaphoreType.DMA((2 * TOGETHER,)),
            pltpu.SemaphoreType.DMA((COARSE, len(split))),
        ],
        compiler_params=pltpu.CompilerParams(vmem_limit_bytes=VMEM_BYTES),
        cost_estimate=pl.CostEstimate(
            flops=16 * 2 * 3 * F * F * 4 * count, bytes_accessed=32 * F * count * 4, transcendentals=0
        ),
        name="spectra",
    )(flags, voltages, taps, table)


def correlate_kernel(scale, base, tiles_ref, own1, own2, other1, other2, *rest):
    out_hbm, heads, tails, groups, made, in_sem, out_sem = rest[-7:]
    mine = lax.axis_index("narrow")
    channels = heads.shape[0]
    count = out_hbm.shape[0]
    slots = made.shape[0]
    head = heads.shape[-1]

    def incoming(j):
        head_rows = pl.ds(16 * (base + j), 16)
        rows = pl.ds(16 * j, 16)
        copies = []
        for side, (first, second) in enumerate(((own1, own2), (other1, other2))):
            copies.append(
                pltpu.make_async_copy(first.at[:, head_rows, :], heads.at[j, side], in_sem.at[j, side, 0])
            )
            copies.append(
                pltpu.make_async_copy(second.at[:, rows, :], tails.at[j, side], in_sem.at[j, side, 1])
            )
        return copies

    def outgoing(j, t):
        slot = (j * count + t) % slots
        return pltpu.make_async_copy(
            made.at[slot], out_hbm.at[t, base + j], out_sem.at[slot]
        )

    for copy in incoming(0):
        copy.start()
    dims = (((1,), (1,)), ((), ()))
    for j in range(channels):
        for copy in incoming(j):
            copy.wait()
        if j + 1 < channels:
            for copy in incoming(j + 1):
                copy.start()
        hold = j % 2
        for side in range(2):
            half = mine if side == 0 else 1 - mine
            for part in range(2):
                sources = slice(part * 32, part * 32 + 32)
                for at, held in ((0, heads), (head, tails)):
                    value = held[j, side, sources].astype(jnp.float32)
                    size = value.shape[2]
                    for which in range(2):
                        piece = value[:, which * 8 : which * 8 + 8, :].reshape(256, size)
                        groups[hold, half * 2 + part, which * 256 : which * 256 + 256, at : at + size] = (
                            piece.astype(jnp.bfloat16)
                        )
        for t in range(count):
            n = j * count + t
            slot = n % slots
            rows = groups[hold, tiles_ref[0, t]]
            column = tiles_ref[1, t]
            with_real = lax.dot_general(
                rows, groups[hold, column, 0:256, :], dims, preferred_element_type=jnp.float32
            )
            with_imag = lax.dot_general(
                rows, groups[hold, column, 256:512, :], dims, preferred_element_type=jnp.float32
            )
            real = (with_real[0:256] + with_imag[256:512]) * scale
            imag = (with_real[256:512] - with_imag[0:256]) * scale
            if n >= slots:
                outgoing((n - slots) // count, (n - slots) % count).wait()
            for side in range(2):
                lanes = slice(side * LANES, side * LANES + LANES)
                made[slot, pl.ds(2 * side, 256, stride=4), :] = real[:, lanes]
                made[slot, pl.ds(2 * side + 1, 256, stride=4), :] = imag[:, lanes]
            outgoing(j, t).start()
    for n in range(max(channels * count - slots, 0), channels * count):
        outgoing(n // count, n % count).wait()


def correlate(tiles, own1, own2, other1, other2, base, before):
    head, tail = own1.shape[-1], own2.shape[-1]
    spectra_count = head + tail
    count = tiles.shape[1]
    smem, hbm = (pl.BlockSpec(memory_space=m) for m in (pltpu.SMEM, pl.ANY))
    operands = [tiles, own1, own2, other1, other2]
    aliases = {}
    if before is not None:
        operands.append(before)
        aliases = {5: 0}
    channels = own2.shape[1] // 16
    return pl.pallas_call(
        functools.partial(correlate_kernel, 1.0 / spectra_count, base),
        out_shape=jax.ShapeDtypeStruct((count, PER, 1024, LANES), jnp.float32),
        in_specs=[smem] + [hbm] * (len(operands) - 1),
        out_specs=hbm,
        scratch_shapes=[
            pltpu.VMEM((channels, 2, WIDE, 16, head), jnp.bfloat16),
            pltpu.VMEM((channels, 2, WIDE, 16, tail), jnp.bfloat16),
            pltpu.VMEM((2, 4, 512, spectra_count), jnp.bfloat16),
            pltpu.VMEM((MADE, 1024, LANES), jnp.float32),
            pltpu.SemaphoreType.DMA((channels, 2, 2)),
            pltpu.SemaphoreType.DMA((MADE,)),
        ],
        input_output_aliases=aliases,
        compiler_params=pltpu.CompilerParams(vmem_limit_bytes=VMEM_BYTES),
        cost_estimate=pl.CostEstimate(
            flops=5 * channels * 8 * 256 * 256 * spectra_count, bytes_accessed=20 * 2**20, transcendentals=0
        ),
        name="correlate",
    )(*operands)


def body(voltages, flags, tiles):
    spectra_count = voltages.shape[3] - TAPS + 1
    count = tiles.shape[0]
    taps = jnp.asarray(filter_table())
    table = jnp.asarray(transform_table())
    by_time = jnp.transpose(voltages, (0, 1, 2, 4, 3))
    pairs = jnp.transpose(tiles)

    def exchange(value):
        return lax.all_to_all(value, "wide", split_axis=0, concat_axis=0, tiled=True)

    def swap(value):
        return lax.ppermute(value, "narrow", [(0, 1), (1, 0)])

    (head,) = spectra(flags, by_time, taps, table, 0, HEAD, (PER,))
    head, by_time = lax.optimization_barrier((head, by_time))
    own_head = exchange(head)
    tails = spectra(flags, by_time, taps, table, HEAD, spectra_count - HEAD, SPLIT)
    own_head, first, second = lax.optimization_barrier((own_head, *tails))
    own_first = exchange(first)
    other_head = swap(own_head)
    own_first, second = lax.optimization_barrier((own_first, second))
    own_second = exchange(second)
    other_first = swap(own_first)
    out = correlate(pairs, own_head, own_first, other_head, other_first, 0, None)
    own_second, out = lax.optimization_barrier((own_second, out))
    other_second = swap(own_second)
    out = correlate(pairs, own_head, own_second, other_head, other_second, SPLIT[0], out)
    out = out.reshape(count, PER, 512, 2, LANES)
    out = jnp.transpose(out, (0, 1, 3, 2, 4))
    return out.reshape(count, PER, 2, 512 * LANES)


def solution(mesh):
    return jax.shard_map(
        body,
        mesh=mesh,
        in_specs=(P(("narrow", "wide"), None, None, None, None), P(), P("narrow", None)),
        out_specs=P("narrow", "wide", None, None),
        check_vma=False,
    )
```

```python
import functools

import jax
import jax.numpy as jnp
import numpy as np
from jax import lax
from jax.experimental import pallas as pl
from jax.experimental.pallas import tpu as pltpu
from jax.sharding import PartitionSpec as P

F = 192
TAPS = 12
COARSE = 2
HEAD = 256
WIDE = 64
LOCAL = 8
PER = 6
LANES = 128
MADE = 8
CORRELATE_BYTES = 26 * 2**20
TOGETHER = 4
PIECES = 1
SPLIT = (4, 2)
VMEM_BYTES = 60 * 2**20


def prototype():
    length = TAPS * F
    sample = np.arange(length, dtype=np.float64)
    centre = (length - 1) / 2.0
    taper = np.sinc((sample - centre) / F)
    window = 0.5 - 0.5 * np.cos(2.0 * np.pi * (sample + 0.5) / length)
    shaped = taper * window
    shaped = shaped * np.sqrt(F / np.sum(shaped * shaped))
    return shaped.reshape(TAPS, F)


def filter_table():
    taps = prototype().astype(np.float32)
    both = np.concatenate([taps, taps], axis=1)
    return np.ascontiguousarray(np.broadcast_to(both[:, None, :], (TAPS, 8, 2 * F)))


def transform_table():
    k = np.arange(F)
    angle = 2.0 * np.pi * ((k[:, None] * k[None, :]) % F) / F
    cosine, sine = np.cos(angle), np.sin(angle)
    real = np.concatenate([cosine, sine], axis=1)
    imag = np.concatenate([-sine, cosine], axis=1)
    rows = np.stack([real, imag], axis=1).reshape(2 * F, 2 * F) / np.sqrt(float(F))
    rows = rows.astype(np.float32)
    high = rows.astype(jnp.bfloat16)
    low = (rows - high.astype(np.float32)).astype(jnp.bfloat16)
    return np.concatenate([high, high, low], axis=1)


def spectra_kernel(first, count, split, flags_ref, volt_ref, taps_ref, table_ref, *rest):
    parts = len(split)
    outs, results = rest[:parts], rest[parts : 2 * parts]
    scratch = rest[2 * parts :]
    series, framed = scratch[:TOGETHER], scratch[TOGETHER : 2 * TOGETHER]
    volts, turned, in_sem, out_sem = scratch[2 * TOGETHER :]
    device = lax.axis_index("narrow") * WIDE + lax.axis_index("wide")
    slots = volts.shape[0]
    width = count + LANES
    total = COARSE * LOCAL
    span = volts.shape[-1]

    def incoming(n):
        slot = lax.rem(n, slots)
        source = volt_ref.at[lax.rem(n, LOCAL), n // LOCAL]
        if span < volt_ref.shape[-1]:
            source = source.at[:, :, pl.ds(0, span)]
        return pltpu.make_async_copy(source, volts.at[slot], in_sem.at[slot])

    def outgoing(c):
        half = WIDE // COARSE
        return [
            pltpu.make_async_copy(held.at[c], out.at[pl.ds(c * half, half)], out_sem.at[c, which])
            for which, (held, out) in enumerate(zip(results, outs))
        ]

    def transform(slot, i, series, framed):
        keep = (1 - flags_ref[(device * LOCAL + i) // 2]).astype(jnp.float32)
        for tile in range(width // LANES):
            start = first + tile * LANES
            stop = min(start + LANES, span)
            pieces = [volts[slot, p, :, start:stop].astype(jnp.float32) for p in range(2)]
            rows = jnp.concatenate(pieces, axis=0)
            for column in range(3):
                series[column, tile * LANES : tile * LANES + stop - start, :] = rows[
                    column * LANES : (column + 1) * LANES
                ].T
        for column in range(3):
            lanes = slice(column * LANES, (column + 1) * LANES)
            taps = [taps_ref[m, :, lanes] for m in range(TAPS)]
            for start in range(0, count, 64):
                value = None
                for m in range(TAPS):
                    tap = jnp.concatenate([taps[m]] * 8, axis=0)
                    term = tap * series[column, start + m : start + m + 64, :]
                    value = term if value is None else value + term
                top = value.astype(jnp.bfloat16)
                rest_part = (value - top.astype(jnp.float32)).astype(jnp.bfloat16)
                for third, half in enumerate((top, rest_part, top)):
                    at = third * 2 * F + column * LANES
                    framed[start : start + 64, at : at + LANES] = half
        product = lax.dot_general(
            table_ref[...], framed[...], (((1,), (1,)), ((), ())), preferred_element_type=jnp.float32
        )
        product = product * keep
        for tile in range(count // LANES):
            turned[tile, pl.ds(i, 2 * F, stride=LOCAL), :] = product[
                :, tile * LANES : (tile + 1) * LANES
            ]

    def step(q, carry):
        n = q * TOGETHER
        c = n // LOCAL

        @pl.when(n + TOGETHER < total)
        def _():
            for k in range(TOGETHER):
                incoming(n + TOGETHER + k).start()

        for k in range(TOGETHER):
            incoming(n + k).wait()
        for k in range(TOGETHER):
            transform(lax.rem(n + k, slots), lax.rem(n, LOCAL) + k, series[k], framed[k])

        @pl.when(lax.rem(n, LOCAL) == LOCAL - TOGETHER)
        def _():
            for tile in range(count // LANES):
                value = turned[tile].astype(jnp.bfloat16)
                value = value.reshape(WIDE // COARSE, PER * 2 * LOCAL, LANES)
                lanes = slice(tile * LANES, (tile + 1) * LANES)
                at = 0
                for held, channels in zip(results, split):
                    rows = channels * 2 * LOCAL
                    held[c, :, :, lanes] = value[:, at : at + rows, :]
                    at += rows
            for copy in outgoing(c):
                copy.start()

        return carry

    for k in range(TOGETHER):
        incoming(k).start()
    lax.fori_loop(0, total // TOGETHER, step, 0)
    for c in range(COARSE):
        for copy in outgoing(c):
            copy.wait()


def spectra(flags, voltages, taps, table, first, count, split):
    half = WIDE // COARSE
    reach = first + count + TAPS - 1
    span = min(-(-reach // LANES) * LANES, voltages.shape[-1])
    sizes = [(channels * 2 * LOCAL, count) for channels in split]
    smem, vmem, hbm = (
        pl.BlockSpec(memory_space=m) for m in (pltpu.SMEM, pltpu.VMEM, pl.ANY)
    )
    return pl.pallas_call(
        functools.partial(spectra_kernel, first, count, split),
        out_shape=[jax.ShapeDtypeStruct((WIDE,) + size, jnp.bfloat16) for size in sizes],
        in_specs=[smem, hbm, vmem, vmem],
        out_specs=[hbm] * len(split),
        scratch_shapes=[pltpu.VMEM((COARSE, half) + size, jnp.bfloat16) for size in sizes]
        + [pltpu.VMEM((3, count + LANES, LANES), jnp.float32)] * TOGETHER
        + [pltpu.VMEM((count, 6 * F), jnp.bfloat16)] * TOGETHER
        + [
            pltpu.VMEM((2 * TOGETHER, 2, F, span), jnp.bfloat16),
            pltpu.VMEM((count // LANES, 2 * F * LOCAL, LANES), jnp.float32),
            pltpu.SemaphoreType.DMA((2 * TOGETHER,)),
            pltpu.SemaphoreType.DMA((COARSE, len(split))),
        ],
        compiler_params=pltpu.CompilerParams(vmem_limit_bytes=VMEM_BYTES),
        cost_estimate=pl.CostEstimate(
            flops=16 * 2 * 3 * F * F * 4 * count, bytes_accessed=32 * F * count * 4, transcendentals=0
        ),
        name="spectra",
    )(flags, voltages, taps, table)


def correlate_kernel(scale, base, tiles_ref, own1, own2, other1, other2, *rest):
    out_hbm, heads, tails, groups, made, in_sem, out_sem = rest[-7:]
    mine = lax.axis_index("narrow")
    channels = heads.shape[0]
    count = out_hbm.shape[0]
    slots = made.shape[0]
    head = heads.shape[-1]

    def incoming(j):
        head_rows = pl.ds(16 * (base + j), 16)
        rows = pl.ds(16 * j, 16)
        copies = []
        for side, (first, second) in enumerate(((own1, own2), (other1, other2))):
            for piece in range(PIECES):
                some = pl.ds(piece * (WIDE // PIECES), WIDE // PIECES)
                for which, (source, there, held) in enumerate(
                    ((first, head_rows, heads), (second, rows, tails))
                ):
                    copies.append(
                        pltpu.make_async_copy(
                            source.at[some, there, :], held.at[j, side, some], in_sem.at[j, side, which, piece]
                        )
                    )
        return copies

    def outgoing(j, t):
        slot = (j * count + t) % slots
        return pltpu.make_async_copy(
            made.at[slot], out_hbm.at[t, base + j], out_sem.at[slot]
        )

    for copy in incoming(0):
        copy.start()
    dims = (((1,), (1,)), ((), ()))
    for j in range(channels):
        for copy in incoming(j):
            copy.wait()
        if j + 1 < channels:
            for copy in incoming(j + 1):
                copy.start()
        hold = j % 2
        for side in range(2):
            half = mine if side == 0 else 1 - mine
            for part in range(2):
                sources = slice(part * 32, part * 32 + 32)
                for at, held in ((0, heads), (head, tails)):
                    value = held[j, side, sources].astype(jnp.float32)
                    size = value.shape[2]
                    for which in range(2):
                        piece = value[:, which * 8 : which * 8 + 8, :].reshape(256, size)
                        groups[hold, half * 2 + part, which * 256 : which * 256 + 256, at : at + size] = (
                            piece.astype(jnp.bfloat16)
                        )
        for t in range(count):
            n = j * count + t
            slot = n % slots
            rows = groups[hold, tiles_ref[0, t]]
            column = tiles_ref[1, t]
            with_real = lax.dot_general(
                rows, groups[hold, column, 0:256, :], dims, preferred_element_type=jnp.float32
            )
            with_imag = lax.dot_general(
                rows, groups[hold, column, 256:512, :], dims, preferred_element_type=jnp.float32
            )
            real = (with_real[0:256] + with_imag[256:512]) * scale
            imag = (with_real[256:512] - with_imag[0:256]) * scale
            if n >= slots:
                outgoing((n - slots) // count, (n - slots) % count).wait()
            for side in range(2):
                lanes = slice(side * LANES, side * LANES + LANES)
                made[slot, pl.ds(2 * side, 256, stride=4), :] = real[:, lanes]
                made[slot, pl.ds(2 * side + 1, 256, stride=4), :] = imag[:, lanes]
            outgoing(j, t).start()
    for n in range(max(channels * count - slots, 0), channels * count):
        outgoing(n // count, n % count).wait()


def correlate(tiles, own1, own2, other1, other2, base, before):
    head, tail = own1.shape[-1], own2.shape[-1]
    spectra_count = head + tail
    count = tiles.shape[1]
    smem, hbm = (pl.BlockSpec(memory_space=m) for m in (pltpu.SMEM, pl.ANY))
    operands = [tiles, own1, own2, other1, other2]
    aliases = {}
    if before is not None:
        operands.append(before)
        aliases = {5: 0}
    channels = own2.shape[1] // 16
    return pl.pallas_call(
        functools.partial(correlate_kernel, 1.0 / spectra_count, base),
        out_shape=jax.ShapeDtypeStruct((count, PER, 1024, LANES), jnp.float32),
        in_specs=[smem] + [hbm] * (len(operands) - 1),
        out_specs=hbm,
        scratch_shapes=[
            pltpu.VMEM((channels, 2, WIDE, 16, head), jnp.bfloat16),
            pltpu.VMEM((channels, 2, WIDE, 16, tail), jnp.bfloat16),
            pltpu.VMEM((2, 4, 512, spectra_count), jnp.bfloat16),
            pltpu.VMEM((MADE, 1024, LANES), jnp.float32),
            pltpu.SemaphoreType.DMA((channels, 2, 2, PIECES)),
            pltpu.SemaphoreType.DMA((MADE,)),
        ],
        input_output_aliases=aliases,
        compiler_params=pltpu.CompilerParams(vmem_limit_bytes=CORRELATE_BYTES),
        cost_estimate=pl.CostEstimate(
            flops=5 * channels * 8 * 256 * 256 * spectra_count, bytes_accessed=20 * 2**20, transcendentals=0
        ),
        name="correlate",
    )(*operands)


def body(voltages, flags, tiles):
    spectra_count = voltages.shape[3] - TAPS + 1
    count = tiles.shape[0]
    taps = jnp.asarray(filter_table())
    table = jnp.asarray(transform_table())
    by_time = jnp.transpose(voltages, (0, 1, 2, 4, 3))
    pairs = jnp.transpose(tiles)

    def exchange(value):
        return lax.all_to_all(value, "wide", split_axis=0, concat_axis=0, tiled=True)

    def swap(value):
        return lax.ppermute(value, "narrow", [(0, 1), (1, 0)])

    (head,) = spectra(flags, by_time, taps, table, 0, HEAD, (PER,))
    head, by_time = lax.optimization_barrier((head, by_time))
    own_head = exchange(head)
    tails = spectra(flags, by_time, taps, table, HEAD, spectra_count - HEAD, SPLIT)
    own_head, first, second = lax.optimization_barrier((own_head, *tails))
    own_first = exchange(first)
    other_head = swap(own_head)
    own_first, second = lax.optimization_barrier((own_first, second))
    own_second = exchange(second)
    other_first = swap(own_first)
    out = correlate(pairs, own_head, own_first, other_head, other_first, 0, None)
    own_second, out = lax.optimization_barrier((own_second, out))
    other_second = swap(own_second)
    out = correlate(pairs, own_head, own_second, other_head, other_second, SPLIT[0], out)
    out = out.reshape(count, PER, 512, 2, LANES)
    out = jnp.transpose(out, (0, 1, 3, 2, 4))
    return out.reshape(count, PER, 2, 512 * LANES)


def solution(mesh):
    return jax.shard_map(
        body,
        mesh=mesh,
        in_specs=(P(("narrow", "wide"), None, None, None, None), P(), P("narrow", None)),
        out_specs=P("narrow", "wide", None, None),
        check_vma=False,
    )
```

```python
import functools

import jax
import jax.numpy as jnp
import numpy as np
from jax import lax
from jax.experimental import pallas as pl
from jax.experimental.pallas import tpu as pltpu
from jax.sharding import PartitionSpec as P

F = 192
TAPS = 12
COARSE = 2
HEAD = 256
WIDE = 64
LOCAL = 8
PER = 6
LANES = 128
MADE = 8
CORRELATE_BYTES = 26 * 2**20
TOGETHER = 4
PIECES = 1
SPLIT = (4, 2)
VMEM_BYTES = 60 * 2**20


def prototype():
    length = TAPS * F
    sample = np.arange(length, dtype=np.float64)
    centre = (length - 1) / 2.0
    taper = np.sinc((sample - centre) / F)
    window = 0.5 - 0.5 * np.cos(2.0 * np.pi * (sample + 0.5) / length)
    shaped = taper * window
    shaped = shaped * np.sqrt(F / np.sum(shaped * shaped))
    return shaped.reshape(TAPS, F)


def filter_table():
    taps = prototype().astype(np.float32)
    both = np.concatenate([taps, taps], axis=1)
    return np.ascontiguousarray(np.broadcast_to(both[:, None, :], (TAPS, 8, 2 * F)))


def transform_table():
    k = np.arange(F)
    angle = 2.0 * np.pi * ((k[:, None] * k[None, :]) % F) / F
    cosine, sine = np.cos(angle), np.sin(angle)
    real = np.concatenate([cosine, sine], axis=1)
    imag = np.concatenate([-sine, cosine], axis=1)
    rows = np.stack([real, imag], axis=1).reshape(2 * F, 2 * F) / np.sqrt(float(F))
    rows = rows.astype(np.float32)
    high = rows.astype(jnp.bfloat16)
    low = (rows - high.astype(np.float32)).astype(jnp.bfloat16)
    return np.concatenate([high, high, low], axis=1)


def spectra_kernel(first, count, split, flags_ref, volt_ref, taps_ref, table_ref, *rest):
    parts = len(split)
    outs, results = rest[:parts], rest[parts : 2 * parts]
    scratch = rest[2 * parts :]
    series, framed = scratch[:TOGETHER], scratch[TOGETHER : 2 * TOGETHER]
    volts, turned, in_sem, out_sem = scratch[2 * TOGETHER :]
    device = lax.axis_index("narrow") * WIDE + lax.axis_index("wide")
    slots = volts.shape[0]
    width = count + LANES
    total = COARSE * LOCAL
    span = volts.shape[-1]

    def incoming(n):
        slot = lax.rem(n, slots)
        source = volt_ref.at[lax.rem(n, LOCAL), n // LOCAL]
        if span < volt_ref.shape[-1]:
            source = source.at[:, :, pl.ds(0, span)]
        return pltpu.make_async_copy(source, volts.at[slot], in_sem.at[slot])

    def outgoing(c):
        half = WIDE // COARSE
        return [
            pltpu.make_async_copy(held.at[c], out.at[pl.ds(c * half, half)], out_sem.at[c, which])
            for which, (held, out) in enumerate(zip(results, outs))
        ]

    def transform(slot, i, series, framed):
        keep = (1 - flags_ref[(device * LOCAL + i) // 2]).astype(jnp.float32)
        for tile in range(width // LANES):
            start = first + tile * LANES
            stop = min(start + LANES, span)
            pieces = [volts[slot, p, :, start:stop].astype(jnp.float32) for p in range(2)]
            rows = jnp.concatenate(pieces, axis=0)
            for column in range(3):
                series[column, tile * LANES : tile * LANES + stop - start, :] = rows[
                    column * LANES : (column + 1) * LANES
                ].T
        for column in range(3):
            lanes = slice(column * LANES, (column + 1) * LANES)
            taps = [taps_ref[m, :, lanes] for m in range(TAPS)]
            for start in range(0, count, 64):
                value = None
                for m in range(TAPS):
                    tap = jnp.concatenate([taps[m]] * 8, axis=0)
                    term = tap * series[column, start + m : start + m + 64, :]
                    value = term if value is None else value + term
                top = value.astype(jnp.bfloat16)
                rest_part = (value - top.astype(jnp.float32)).astype(jnp.bfloat16)
                for third, half in enumerate((top, rest_part, top)):
                    at = third * 2 * F + column * LANES
                    framed[start : start + 64, at : at + LANES] = half
        product = lax.dot_general(
            framed[...], table_ref[...], (((1,), (1,)), ((), ())), preferred_element_type=jnp.float32
        )
        product = product.T * keep
        for tile in range(count // LANES):
            turned[tile, pl.ds(i, 2 * F, stride=LOCAL), :] = product[
                :, tile * LANES : (tile + 1) * LANES
            ]

    def step(q, carry):
        n = q * TOGETHER
        c = n // LOCAL

        @pl.when(n + TOGETHER < total)
        def _():
            for k in range(TOGETHER):
                incoming(n + TOGETHER + k).start()

        for k in range(TOGETHER):
            incoming(n + k).wait()
        for k in range(TOGETHER):
            transform(lax.rem(n + k, slots), lax.rem(n, LOCAL) + k, series[k], framed[k])

        @pl.when(lax.rem(n, LOCAL) == LOCAL - TOGETHER)
        def _():
            for tile in range(count // LANES):
                value = turned[tile].astype(jnp.bfloat16)
                value = value.reshape(WIDE // COARSE, PER * 2 * LOCAL, LANES)
                lanes = slice(tile * LANES, (tile + 1) * LANES)
                at = 0
                for held, channels in zip(results, split):
                    rows = channels * 2 * LOCAL
                    held[c, :, :, lanes] = value[:, at : at + rows, :]
                    at += rows
            for copy in outgoing(c):
                copy.start()

        return carry

    for k in range(TOGETHER):
        incoming(k).start()
    lax.fori_loop(0, total // TOGETHER, step, 0)
    for c in range(COARSE):
        for copy in outgoing(c):
            copy.wait()


def spectra(flags, voltages, taps, table, first, count, split):
    half = WIDE // COARSE
    reach = first + count + TAPS - 1
    span = min(-(-reach // LANES) * LANES, voltages.shape[-1])
    sizes = [(channels * 2 * LOCAL, count) for channels in split]
    smem, vmem, hbm = (
        pl.BlockSpec(memory_space=m) for m in (pltpu.SMEM, pltpu.VMEM, pl.ANY)
    )
    return pl.pallas_call(
        functools.partial(spectra_kernel, first, count, split),
        out_shape=[jax.ShapeDtypeStruct((WIDE,) + size, jnp.bfloat16) for size in sizes],
        in_specs=[smem, hbm, vmem, vmem],
        out_specs=[hbm] * len(split),
        scratch_shapes=[pltpu.VMEM((COARSE, half) + size, jnp.bfloat16) for size in sizes]
        + [pltpu.VMEM((3, count + LANES, LANES), jnp.float32)] * TOGETHER
        + [pltpu.VMEM((count, 6 * F), jnp.bfloat16)] * TOGETHER
        + [
            pltpu.VMEM((2 * TOGETHER, 2, F, span), jnp.bfloat16),
            pltpu.VMEM((count // LANES, 2 * F * LOCAL, LANES), jnp.float32),
            pltpu.SemaphoreType.DMA((2 * TOGETHER,)),
            pltpu.SemaphoreType.DMA((COARSE, len(split))),
        ],
        compiler_params=pltpu.CompilerParams(vmem_limit_bytes=VMEM_BYTES),
        cost_estimate=pl.CostEstimate(
            flops=16 * 2 * 3 * F * F * 4 * count, bytes_accessed=32 * F * count * 4, transcendentals=0
        ),
        name="spectra",
    )(flags, voltages, taps, table)


def correlate_kernel(scale, base, tiles_ref, own1, own2, other1, other2, *rest):
    out_hbm, heads, tails, groups, made, in_sem, out_sem = rest[-7:]
    mine = lax.axis_index("narrow")
    channels = heads.shape[0]
    count = out_hbm.shape[0]
    slots = made.shape[0]
    head = heads.shape[-1]

    def incoming(j):
        head_rows = pl.ds(16 * (base + j), 16)
        rows = pl.ds(16 * j, 16)
        copies = []
        for side, (first, second) in enumerate(((own1, own2), (other1, other2))):
            for piece in range(PIECES):
                some = pl.ds(piece * (WIDE // PIECES), WIDE // PIECES)
                for which, (source, there, held) in enumerate(
                    ((first, head_rows, heads), (second, rows, tails))
                ):
                    copies.append(
                        pltpu.make_async_copy(
                            source.at[some, there, :], held.at[j, side, some], in_sem.at[j, side, which, piece]
                        )
                    )
        return copies

    def outgoing(j, t):
        slot = (j * count + t) % slots
        return pltpu.make_async_copy(
            made.at[slot], out_hbm.at[t, base + j], out_sem.at[slot]
        )

    for copy in incoming(0):
        copy.start()
    dims = (((1,), (1,)), ((), ()))
    for j in range(channels):
        hold = j % 2
        for side in range(2):
            for copy in incoming(j)[2 * side * PIECES : 2 * (side + 1) * PIECES]:
                copy.wait()
            if side == 0 and j + 1 < channels:
                for copy in incoming(j + 1):
                    copy.start()
            half = mine if side == 0 else 1 - mine
            for part in range(2):
                sources = slice(part * 32, part * 32 + 32)
                for at, held in ((0, heads), (head, tails)):
                    value = held[j, side, sources].astype(jnp.float32)
                    size = value.shape[2]
                    for which in range(2):
                        piece = value[:, which * 8 : which * 8 + 8, :].reshape(256, size)
                        groups[hold, half * 2 + part, which * 256 : which * 256 + 256, at : at + size] = (
                            piece.astype(jnp.bfloat16)
                        )
        for t in range(count):
            n = j * count + t
            slot = n % slots
            rows = groups[hold, tiles_ref[0, t]]
            column = tiles_ref[1, t]
            with_real = lax.dot_general(
                rows, groups[hold, column, 0:256, :], dims, preferred_element_type=jnp.float32
            )
            with_imag = lax.dot_general(
                rows, groups[hold, column, 256:512, :], dims, preferred_element_type=jnp.float32
            )
            real = (with_real[0:256] + with_imag[256:512]) * scale
            imag = (with_real[256:512] - with_imag[0:256]) * scale
            if n >= slots:
                outgoing((n - slots) // count, (n - slots) % count).wait()
            for side in range(2):
                lanes = slice(side * LANES, side * LANES + LANES)
                made[slot, pl.ds(2 * side, 256, stride=4), :] = real[:, lanes]
                made[slot, pl.ds(2 * side + 1, 256, stride=4), :] = imag[:, lanes]
            outgoing(j, t).start()
    for n in range(max(channels * count - slots, 0), channels * count):
        outgoing(n // count, n % count).wait()


def correlate(tiles, own1, own2, other1, other2, base, before):
    head, tail = own1.shape[-1], own2.shape[-1]
    spectra_count = head + tail
    count = tiles.shape[1]
    smem, hbm = (pl.BlockSpec(memory_space=m) for m in (pltpu.SMEM, pl.ANY))
    operands = [tiles, own1, own2, other1, other2]
    aliases = {}
    if before is not None:
        operands.append(before)
        aliases = {5: 0}
    channels = own2.shape[1] // 16
    return pl.pallas_call(
        functools.partial(correlate_kernel, 1.0 / spectra_count, base),
        out_shape=jax.ShapeDtypeStruct((count, PER, 1024, LANES), jnp.float32),
        in_specs=[smem] + [hbm] * (len(operands) - 1),
        out_specs=hbm,
        scratch_shapes=[
            pltpu.VMEM((channels, 2, WIDE, 16, head), jnp.bfloat16),
            pltpu.VMEM((channels, 2, WIDE, 16, tail), jnp.bfloat16),
            pltpu.VMEM((2, 4, 512, spectra_count), jnp.bfloat16),
            pltpu.VMEM((MADE, 1024, LANES), jnp.float32),
            pltpu.SemaphoreType.DMA((channels, 2, 2, PIECES)),
            pltpu.SemaphoreType.DMA((MADE,)),
        ],
        input_output_aliases=aliases,
        compiler_params=pltpu.CompilerParams(vmem_limit_bytes=CORRELATE_BYTES),
        cost_estimate=pl.CostEstimate(
            flops=5 * channels * 8 * 256 * 256 * spectra_count, bytes_accessed=20 * 2**20, transcendentals=0
        ),
        name="correlate",
    )(*operands)


def body(voltages, flags, tiles):
    spectra_count = voltages.shape[3] - TAPS + 1
    count = tiles.shape[0]
    taps = jnp.asarray(filter_table())
    table = jnp.asarray(transform_table())
    by_time = jnp.transpose(voltages, (0, 1, 2, 4, 3))
    pairs = jnp.transpose(tiles)

    def exchange(value):
        return lax.all_to_all(value, "wide", split_axis=0, concat_axis=0, tiled=True)

    def swap(value):
        return lax.ppermute(value, "narrow", [(0, 1), (1, 0)])

    (head,) = spectra(flags, by_time, taps, table, 0, HEAD, (PER,))
    head, by_time = lax.optimization_barrier((head, by_time))
    own_head = exchange(head)
    tails = spectra(flags, by_time, taps, table, HEAD, spectra_count - HEAD, SPLIT)
    own_head, first, second = lax.optimization_barrier((own_head, *tails))
    own_first = exchange(first)
    other_head = swap(own_head)
    own_first, second = lax.optimization_barrier((own_first, second))
    own_second = exchange(second)
    other_first = swap(own_first)
    out = correlate(pairs, own_head, own_first, other_head, other_first, 0, None)
    own_second, out = lax.optimization_barrier((own_second, out))
    other_second = swap(own_second)
    out = correlate(pairs, own_head, own_second, other_head, other_second, SPLIT[0], out)
    out = out.reshape(count, PER, 512, 2, LANES)
    out = jnp.transpose(out, (0, 1, 3, 2, 4))
    return out.reshape(count, PER, 2, 512 * LANES)


def solution(mesh):
    return jax.shard_map(
        body,
        mesh=mesh,
        in_specs=(P(("narrow", "wide"), None, None, None, None), P(), P("narrow", None)),
        out_specs=P("narrow", "wide", None, None),
        check_vma=False,
    )
```
